32 devices in a mesh: gx: 4 (over x, core), gy: 8 (over z, y).
Axes of the slice: x: 2, y: 2, z: 4, core: 2. Of those that a mesh axis runs over, the one named last changes fastest.
Arguments:
- queries: bfloat16 [4096, 2048], P(('gx', 'gy')), may hold values from -100 to 100
- keys_local: bfloat16 [4096, 2048], P(('gx', 'gy')), may hold values from -5 to 5
- values_local: bfloat16 [4096, 2048], P(('gx', 'gy')), may hold values from -5 to 5
- mem_keys: bfloat16 [16384, 2048], P(('gx', 'gy')), may hold values from -5 to 5
- mem_values: bfloat16 [16384, 2048], P(('gx', 'gy')), may hold values from -5 to 5
- proj: bfloat16 [2048, 2048], P(('gx', 'gy')), may hold values from -0.125 to 0.125
- cotangent: bfloat16 [4096, 2048], P(('gx', 'gy')), may hold values from -6 to 6
- block_list: int32 [32, 16, 3], P(('gx', 'gy')), may hold values from 0 to 31, as said below
Outputs:
- mixed: bfloat16 [4096, 2048], P(('gx', 'gy'))
- grad_proj: float32 [2048, 2048], P(('gx', 'gy'))
- grad_queries: bfloat16 [4096, 2048], P(('gx', 'gy'))
- grad_keys_local: bfloat16 [4096, 2048], P(('gx', 'gy'))
- grad_values_local: bfloat16 [4096, 2048], P(('gx', 'gy'))
- grad_mem_keys: bfloat16 [16384, 2048], P(('gx', 'gy'))
- grad_mem_values: bfloat16 [16384, 2048], P(('gx', 'gy'))
The draws below stay inside these ranges and needn't reach their ends.
Inputs may be any that keep to these rules, and one draw needn't show every extreme that they name: `block_list`: query blocks of gx index i belong to document i. Among the requests of the 1 query block of one device, exactly 8 (block, head) pairs name blocks of each of 6 of the document's memory devices and none name the others' blocks, where memory device j of the document holds its blocks j * 4 to j * 4 + 3. The 3 blocks of one query block and head are distinct.
All inputs are finite; a program needn't handle non-finite values.
Results may differ from the reference program's by a relative error of at most 0.009.
Values may be sent and summed in bfloat16 or wider, within the bound.
A program may use at most 128 MiB of HBM per device.

```python
import jax
import jax.numpy as jnp
from jax import lax

D = 2048
H = 16
DH = 128
BLK = 128
KB = 3
QB = 1
MB_DEV = 4
HD = 2048
TOKENS = 4096
QBLK = 32
DOCS = 4
BPD = 32
MEM = 16384
ITEMS = 48


def draw_queries(key, part):
    key = jax.random.fold_in(key, 11)
    return jnp.clip(jax.random.normal(key, (TOKENS, HD), jnp.float32), -4.5, 4.5).astype(jnp.bfloat16)


def draw_keys_local(key, part):
    key = jax.random.fold_in(key, 12)
    return jnp.clip(jax.random.normal(key, (TOKENS, HD), jnp.float32), -4.5, 4.5).astype(jnp.bfloat16)


def draw_block_list(key, part):
    key = jax.random.fold_in(key, 21)
    senders = QBLK // QB
    row_devices = BPD // MB_DEV
    capacity = ITEMS // (row_devices - row_devices // 4)
    shift_key, local_key = jax.random.split(key)
    shifts = jax.random.randint(shift_key, (senders, 1, 1, 1), 0, row_devices)
    shape = (senders, QB, H, KB)
    block_index = lax.broadcasted_iota(jnp.int32, shape, 1)
    head_index = lax.broadcasted_iota(jnp.int32, shape, 2)
    pick_index = lax.broadcasted_iota(jnp.int32, shape, 3)
    serial = pick_index * (QB * H) + block_index * H + head_index
    owners = (shifts + serial // capacity) % row_devices
    within = jax.random.randint(local_key, shape, 0, MB_DEV)
    return (owners * MB_DEV + within).reshape(QBLK, H, KB).astype(jnp.int32)


def levels(stream_key, extent, cuts, low, high):
    loudness, own = 1.0, jax.random.fold_in(stream_key, 6)
    for position, blocks in cuts:
        draws = jnp.exp(jax.random.uniform(jax.random.fold_in(own, position), (blocks,), jnp.float32, low / len(cuts), high / len(cuts)))
        loudness = loudness * jnp.repeat(draws, extent[position] // blocks).reshape([-1 if axis == position else 1 for axis in range(len(extent))])
    return loudness


def scatter_about(rng, shape, scale, limit, shards=(), held_as=jnp.bfloat16):
    values = scale * jax.random.normal(rng, shape, jnp.float32)
    if shards:
        values = values * levels(rng, shape, shards, -0.22, 0.18)
    return jnp.clip(values, -limit, limit).astype(held_as)


def setup_inputs(seed: int = 0) -> dict:
    arg_keys = jax.random.split(jax.random.key(seed), 9)
    queries = draw_queries(jax.random.fold_in(arg_keys[8], 71), 0)
    keys_local = draw_keys_local(jax.random.fold_in(arg_keys[8], 71), 0)
    values_local = scatter_about(arg_keys[2], (TOKENS, HD), 1.0, 5.0, ((0, 32),))
    mem_keys = scatter_about(arg_keys[3], (MEM, HD), 1.0, 5.0, ((0, 32),))
    mem_values = scatter_about(arg_keys[4], (MEM, HD), 1.0, 5.0, ((0, 32),))
    proj = scatter_about(arg_keys[5], (HD, D), HD ** -0.5, 0.125, ((0, 32),))
    cotangent = scatter_about(arg_keys[6], (TOKENS, D), 1.0, 6.0, ((0, 32),))
    block_list = draw_block_list(jax.random.fold_in(arg_keys[8], 71), 0)
    return dict(queries=queries, keys_local=keys_local, values_local=values_local, mem_keys=mem_keys, mem_values=mem_values, proj=proj, cotangent=cotangent, block_list=block_list)


def split_heads(matrix):
    return matrix.reshape(QBLK, BLK, H, DH).transpose(0, 2, 1, 3)


def join_heads(blocks):
    return blocks.transpose(0, 2, 1, 3).reshape(QBLK * BLK, H * DH)


def fetch_blocks(memory4, block_ids):
    head_index = jnp.arange(H, dtype=jnp.int32)[:, None]
    found = memory4[block_ids, :, head_index, :]
    return found.reshape(H, KB * BLK, DH)


def attend_block(query, key_here, value_here, key_mem, value_mem):
    all_keys = jnp.concatenate([key_here, key_mem], axis=1)
    all_values = jnp.concatenate([value_here, value_mem], axis=1)
    score_scale = DH ** -0.5
    scores = jnp.einsum("hqd,hkd->hqk", query.astype(jnp.float32), all_keys.astype(jnp.float32)) * score_scale
    column = jnp.arange(all_keys.shape[1], dtype=jnp.int32)[None, :]
    row_index = jnp.arange(BLK, dtype=jnp.int32)[:, None]
    visible = (column >= BLK) | (column <= row_index)
    scores = jnp.where(visible[None], scores, jnp.float32(-1e30))
    row_max = jnp.max(scores, axis=-1, keepdims=True)
    expo = jnp.exp(scores - row_max)
    probability = expo / jnp.sum(expo, axis=-1, keepdims=True)
    weights_bf = probability.astype(jnp.bfloat16)
    result = jnp.einsum("hqk,hkd->hqd", weights_bf.astype(jnp.float32), all_values.astype(jnp.float32))
    return all_keys, all_values, probability, weights_bf, result.astype(jnp.bfloat16)


def reference(queries, keys_local, values_local, mem_keys, mem_values, proj, cotangent, block_list):
    keys4 = mem_keys.reshape(MEM // BLK, BLK, H, DH)
    values4 = mem_values.reshape(MEM // BLK, BLK, H, DH)
    query_blocks = split_heads(queries)
    key_blocks = split_heads(keys_local)
    value_blocks = split_heads(values_local)
    documents = (jnp.arange(QBLK, dtype=jnp.int32) // (QBLK // DOCS)).astype(jnp.int32)
    block_ids = (documents[:, None, None] * BPD + block_list).astype(jnp.int32)

    def forward_one(inputs):
        query, key_here, value_here, ids = inputs
        outputs = attend_block(query, key_here, value_here, fetch_blocks(keys4, ids), fetch_blocks(values4, ids))
        return outputs[4]

    attended_blocks = lax.map(forward_one, (query_blocks, key_blocks, value_blocks, block_ids))
    attended = join_heads(attended_blocks)
    mixed = jnp.dot(attended, proj, preferred_element_type=jnp.float32).astype(jnp.bfloat16)
    d_attended = jnp.dot(cotangent, proj.T, preferred_element_type=jnp.float32).astype(jnp.bfloat16)
    grad_proj = jnp.dot(attended.T, cotangent, preferred_element_type=jnp.float32) * (TOKENS ** -0.5)
    d_blocks = split_heads(d_attended)
    head_index = jnp.arange(H, dtype=jnp.int32)[:, None]

    def backward_one(carry, inputs):
        grad_keys4, grad_values4 = carry
        query, key_here, value_here, ids, d_out = inputs
        all_keys, all_values, probability, weights_bf, result = attend_block(
            query, key_here, value_here, fetch_blocks(keys4, ids), fetch_blocks(values4, ids))
        d_prob = jnp.einsum("hqd,hkd->hqk", d_out.astype(jnp.float32), all_values.astype(jnp.float32))
        delta = jnp.sum(probability * d_prob, axis=-1, keepdims=True)
        d_score = (probability * (d_prob - delta) * (DH ** -0.5)).astype(jnp.bfloat16)
        grad_query = jnp.einsum("hqk,hkd->hqd", d_score.astype(jnp.float32), all_keys.astype(jnp.float32)).astype(jnp.bfloat16)
        key_terms = jnp.einsum("hqk,hqd->hkd", d_score.astype(jnp.float32), query.astype(jnp.float32))
        value_terms = jnp.einsum("hqk,hqd->hkd", weights_bf.astype(jnp.float32), d_out.astype(jnp.float32))
        mem_key_terms = lax.optimization_barrier(key_terms[:, BLK:].astype(jnp.bfloat16)).astype(jnp.float32)
        mem_value_terms = lax.optimization_barrier(value_terms[:, BLK:].astype(jnp.bfloat16)).astype(jnp.float32)
        grad_keys4 = grad_keys4.at[ids, :, head_index, :].add(mem_key_terms.reshape(H, KB, BLK, DH))
        grad_values4 = grad_values4.at[ids, :, head_index, :].add(mem_value_terms.reshape(H, KB, BLK, DH))
        local_parts = (grad_query, key_terms[:, :BLK].astype(jnp.bfloat16), value_terms[:, :BLK].astype(jnp.bfloat16))
        return (grad_keys4, grad_values4), local_parts

    empty = jnp.zeros((MEM // BLK, BLK, H, DH), jnp.float32)
    sums, local_grads = lax.scan(backward_one, (empty, empty),
                                 (query_blocks, key_blocks, value_blocks, block_ids, d_blocks))
    grad_queries = join_heads(local_grads[0])
    grad_keys_local = join_heads(local_grads[1])
    grad_values_local = join_heads(local_grads[2])
    grad_mem_keys = sums[0].reshape(MEM, HD).astype(jnp.bfloat16)
    grad_mem_values = sums[1].reshape(MEM, HD).astype(jnp.bfloat16)
    return (mixed, grad_proj, grad_queries, grad_keys_local, grad_values_local, grad_mem_keys, grad_mem_values)
```

```python
import functools

import jax
import jax.numpy as jnp
from jax import lax
from jax.experimental import pallas as pl
from jax.experimental.pallas import tpu as pltpu
from jax.sharding import PartitionSpec as P

H = 16
DH = 128
BLK = 128
KB = 3
MB_DEV = 4
HEADS_PER_STEP = 2
VMEM_BYTES = 48 * 1024 * 1024


def params(**extra):
    return pltpu.CompilerParams(vmem_limit_bytes=VMEM_BYTES, **extra)


def block_of(code):
    rows = pl.ds(pl.multiple_of((code // H) * BLK, BLK), BLK)
    columns = pl.ds(pl.multiple_of((code % H) * DH, DH), DH)
    return rows, columns


def gather_kernel(capacity, wanted_ref, keys_ref, values_ref, found_ref):
    base = pl.program_id(0) * capacity

    def body(slot, carry):
        rows, columns = block_of(jnp.maximum(wanted_ref[base + slot], 0))
        found_ref[slot, :, :DH] = keys_ref[rows, columns]
        found_ref[slot, :, DH:] = values_ref[rows, columns]
        return carry

    lax.fori_loop(0, capacity, body, 0)


def gather_blocks(wanted, mem_keys, mem_values, peers, capacity):
    whole = pl.BlockSpec(mem_keys.shape, lambda i, wanted: (0, 0))
    return pl.pallas_call(
        functools.partial(gather_kernel, capacity),
        out_shape=jax.ShapeDtypeStruct((peers * capacity, BLK, 2 * DH), jnp.bfloat16),
        grid_spec=pltpu.PrefetchScalarGridSpec(
            num_scalar_prefetch=1,
            grid=(peers,),
            in_specs=[whole, whole],
            out_specs=pl.BlockSpec((capacity, BLK, 2 * DH), lambda i, wanted: (i, 0, 0)),
        ),
        compiler_params=params(),
    )(wanted, mem_keys, mem_values)


def dot_nt(a, b):
    return lax.dot_general(a, b, (((1,), (1,)), ((), ())), preferred_element_type=jnp.float32)


def dot_tn(a, b):
    return lax.dot_general(a, b, (((0,), (0,)), ((), ())), preferred_element_type=jnp.float32)


def attention_kernel(
    position_ref, q_ref, k_ref, v_ref, do_ref, mem_ref, att_ref, dq_ref, dk_ref, dv_ref, out_ref
):
    scale = DH ** (-0.5)
    step = pl.program_id(0)
    column = lax.broadcasted_iota(jnp.int32, (BLK, (KB + 1) * BLK), 1)
    row = lax.broadcasted_iota(jnp.int32, (BLK, (KB + 1) * BLK), 0)
    visible = (column >= BLK) | (column <= row)
    for part in range(HEADS_PER_STEP):
        head = step * HEADS_PER_STEP + part
        here = slice(part * DH, (part + 1) * DH)
        slots = [position_ref[k * H + head] for k in range(KB)]
        q = q_ref[:, here]
        do = do_ref[:, here]
        keys = jnp.concatenate([k_ref[:, here]] + [mem_ref[s, :, :DH] for s in slots], axis=0)
        values = jnp.concatenate([v_ref[:, here]] + [mem_ref[s, :, DH:] for s in slots], axis=0)
        scores = jnp.where(visible, dot_nt(q, keys) * scale, jnp.float32(-1e30))
        expo = jnp.exp(scores - jnp.max(scores, axis=-1, keepdims=True))
        probability = expo / jnp.sum(expo, axis=-1, keepdims=True)
        weights = probability.astype(jnp.bfloat16)
        att_ref[:, here] = jnp.dot(weights, values, preferred_element_type=jnp.float32).astype(
            jnp.bfloat16
        )
        d_prob = dot_nt(do, values)
        delta = jnp.sum(probability * d_prob, axis=-1, keepdims=True)
        d_score = (probability * (d_prob - delta) * scale).astype(jnp.bfloat16)
        dq_ref[:, here] = jnp.dot(d_score, keys, preferred_element_type=jnp.float32).astype(
            jnp.bfloat16
        )
        key_terms = dot_tn(d_score, q).astype(jnp.bfloat16)
        value_terms = dot_tn(weights, do).astype(jnp.bfloat16)
        dk_ref[:, here] = key_terms[:BLK]
        dv_ref[:, here] = value_terms[:BLK]
        for k, slot in enumerate(slots):
            rows = slice((k + 1) * BLK, (k + 2) * BLK)
            out_ref[slot, :, :DH] = key_terms[rows]
            out_ref[slot, :, DH:] = value_terms[rows]


def attend(position, queries, keys_local, values_local, d_attended, returned):
    tokens, features = queries.shape
    heads = pl.BlockSpec((tokens, HEADS_PER_STEP * DH), lambda i, position: (0, i))
    whole = pl.BlockSpec(returned.shape, lambda i, position: (0, 0, 0))
    rows = jax.ShapeDtypeStruct((tokens, features), jnp.bfloat16)
    return pl.pallas_call(
        attention_kernel,
        out_shape=(rows, rows, rows, rows, jax.ShapeDtypeStruct(returned.shape, jnp.bfloat16)),
        grid_spec=pltpu.PrefetchScalarGridSpec(
            num_scalar_prefetch=1,
            grid=(H // HEADS_PER_STEP,),
            in_specs=[heads, heads, heads, heads, whole],
            out_specs=(heads, heads, heads, heads, whole),
        ),
        compiler_params=params(),
    )(position, queries, keys_local, values_local, d_attended, returned)


def collect_kernel(capacity, wanted_ref, incoming_ref, keys_ref, values_ref, key_sum, value_sum):
    step = pl.program_id(0)

    @pl.when(step == 0)
    def _():
        key_sum[...] = jnp.zeros_like(key_sum)
        value_sum[...] = jnp.zeros_like(value_sum)

    def body(slot, carry):
        code = wanted_ref[step * capacity + slot]

        @pl.when(code >= 0)
        def _():
            where = block_of(code)
            key_sum[where] += incoming_ref[slot, :, :DH].astype(jnp.float32)
            value_sum[where] += incoming_ref[slot, :, DH:].astype(jnp.float32)

        return carry

    lax.fori_loop(0, capacity, body, 0)

    @pl.when(step == pl.num_programs(0) - 1)
    def _():
        keys_ref[...] = key_sum[...].astype(jnp.bfloat16)
        values_ref[...] = value_sum[...].astype(jnp.bfloat16)


def collect_terms(wanted, incoming, peers, capacity):
    shape = (MB_DEV * BLK, H * DH)
    whole = pl.BlockSpec(shape, lambda i, wanted: (0, 0))
    table = jax.ShapeDtypeStruct(shape, jnp.bfloat16)
    return pl.pallas_call(
        functools.partial(collect_kernel, capacity),
        out_shape=(table, table),
        grid_spec=pltpu.PrefetchScalarGridSpec(
            num_scalar_prefetch=1,
            grid=(peers,),
            in_specs=[pl.BlockSpec((capacity, BLK, 2 * DH), lambda i, wanted: (i, 0, 0))],
            out_specs=(whole, whole),
            scratch_shapes=[pltpu.VMEM(shape, jnp.float32), pltpu.VMEM(shape, jnp.float32)],
        ),
        compiler_params=params(),
    )(wanted, incoming)


def projection_gradient(attended, cotangent, sizes):
    order = []
    for name in ("gx", "gy"):
        order += [(name, bit) for bit in range(sizes[name].bit_length() - 1)]
    dims = [(name, bit) for name in ("gx", "gy") for bit in reversed(range(sizes[name].bit_length() - 1))]
    tokens, features = attended.shape
    rest = features // (sizes["gx"] * sizes["gy"])
    columns = attended.reshape((tokens,) + (2,) * len(dims) + (rest,))
    total = None
    for place, (name, bit) in enumerate(order):
        axis = dims.index((name, bit))
        mine = (lax.axis_index(name) >> bit) & 1
        pairs = [(i, i ^ (1 << bit)) for i in range(sizes[name])]
        dims = dims[:axis] + dims[axis + 1 :]
        last = place == len(order) - 1
        if total is None:
            shape = (2,) * len(dims) + (rest, cotangent.shape[1])

            def product(which):
                part = lax.dynamic_index_in_dim(columns, which, axis + 1, keepdims=False)
                return dot_tn(part.reshape(tokens, features // 2), cotangent)

            sent = product(1 - mine).astype(jnp.bfloat16).reshape(shape)
            kept = product(mine).reshape(shape)
        else:
            sent = lax.dynamic_index_in_dim(total, 1 - mine, axis, keepdims=False)
            kept = lax.dynamic_index_in_dim(total, mine, axis, keepdims=False).astype(jnp.float32)
        total = kept + lax.ppermute(sent, name, pairs).astype(jnp.float32)
        if not last:
            total = total.astype(jnp.bfloat16)
    return total


def local(sizes, queries, keys_local, values_local, mem_keys, mem_values, proj, cotangent, block_list):
    peers = sizes["gy"]
    item_count = H * KB
    capacity = item_count // (peers - peers // 4)
    slot_count = peers * capacity
    ordered = block_list.reshape(H, KB).T.reshape(item_count)
    item = jnp.arange(item_count, dtype=jnp.int32)
    owners = ordered // MB_DEV
    codes = ordered % MB_DEV * H + item % H
    earlier = (owners[:, None] == owners[None, :]) & (item[None, :] < item[:, None])
    position = owners * capacity + jnp.sum(earlier.astype(jnp.int32), axis=1)
    selector = jnp.arange(slot_count, dtype=jnp.int32)[:, None] == position[None, :]
    request = jnp.sum(jnp.where(selector, codes[None, :] + 1, 0), axis=1) - 1
    wanted = lax.all_to_all(
        request.reshape(peers, capacity), "gy", split_axis=0, concat_axis=0, tiled=True
    ).reshape(slot_count)

    found = gather_blocks(wanted, mem_keys, mem_values, peers, capacity)
    returned = lax.all_to_all(
        found.reshape(peers, capacity, BLK, 2 * DH), "gy", split_axis=0, concat_axis=0, tiled=True
    ).reshape(slot_count, BLK, 2 * DH)

    proj_all = lax.all_gather(proj, ("gx", "gy"), axis=0, tiled=True)
    d_attended = dot_nt(cotangent, proj_all).astype(jnp.bfloat16)

    attended, grad_queries, grad_keys_local, grad_values_local, outgoing = attend(
        position, queries, keys_local, values_local, d_attended, returned
    )
    incoming = lax.all_to_all(
        outgoing.reshape(peers, capacity, BLK, 2 * DH), "gy", split_axis=0, concat_axis=0, tiled=True
    ).reshape(slot_count, BLK, 2 * DH)

    total_tokens = queries.shape[0] * sizes["gx"] * peers
    grad_proj = projection_gradient(attended, cotangent, sizes) * total_tokens ** (-0.5)
    mixed = jnp.dot(attended, proj_all, preferred_element_type=jnp.float32).astype(jnp.bfloat16)

    grad_mem_keys, grad_mem_values = collect_terms(wanted, incoming, peers, capacity)
    return (
        mixed,
        grad_proj,
        grad_queries,
        grad_keys_local,
        grad_values_local,
        grad_mem_keys,
        grad_mem_values,
    )


def solution(mesh):
    rows = P(("gx", "gy"), None)
    return jax.shard_map(
        functools.partial(local, dict(mesh.shape)),
        mesh=mesh,
        in_specs=(rows,) * 7 + (P(("gx", "gy"), None, None),),
        out_specs=(rows,) * 7,
        check_vma=False,
    )
```
